512 devices in a mesh: rows: 64 (over x, z), grp: 8 (over y, core).
Axes of the slice: x: 4, y: 4, z: 16, core: 2. Of those that a mesh axis runs over, the one named last changes fastest.
Arguments:
- sample: float32 [524288, 1024], P(('rows', 'grp')), as said below
- test_matrix: float32 [1024, 256], replicated, may hold values from -0.1875 to 0.1875
Outputs:
- basis: float32 [524288, 256], P(('rows', 'grp'))
- factor: float32 [256, 1024], replicated
The draws below stay inside these ranges and needn't reach their ends.
Inputs may be any that keep to these rules, and one draw needn't show every extreme that they name: Every row of the sample has a positive scale and the sample has full column rank on every device.
All inputs are finite; a program needn't handle non-finite values.
Results may differ from the reference program's by a relative error of at most 0.000082.
Values sent between devices are 32-bit elements; how exact they have to be, the bound alone decides.
A program may use at most 64 MiB of HBM per device.

```python
import jax
import jax.numpy as jnp
from jax import lax

D = 1024
RANK = 256
M = 524288


def draw_sample(key, part):
    key = jax.random.fold_in(key, 11)
    first, second, third = jax.random.split(key, 3)
    ramp = jnp.arange(M).astype(jnp.float32) / jnp.float32(max(M - 1, 1))
    noise = jnp.clip(jax.random.normal(first, (M, D), jnp.float32), -5.0, 5.0)
    spread = jnp.log(10.0)
    row_scale = jnp.exp(jax.random.uniform(second, (M, 1), jnp.float32) * spread) * (1.0 + 2.0 * ramp)[:, None]
    col_scale = jnp.exp(jax.random.uniform(third, (1, D), jnp.float32) * spread)
    return noise * row_scale * col_scale / (8.0 * jnp.sqrt(jnp.float32(M)))


def bell_draw(own_key, dims, scale, reach, kind=jnp.bfloat16):
    values = scale * jax.random.normal(own_key, dims, jnp.float32)
    return jnp.clip(values, min=-reach, max=reach).astype(kind)


def setup_inputs(seed: int = 0) -> dict:
    splits = jax.random.split(jax.random.key(seed), 3)
    return {
        "sample": draw_sample(jax.random.fold_in(splits[2], 71), 0),
        "test_matrix": bell_draw(splits[1], (D, RANK), D ** -0.5, 0.1875, jnp.float32),
    }


def reference(sample, test_matrix):
    highest = lax.Precision.HIGHEST
    sketch = jnp.dot(sample, test_matrix, precision=highest)
    gram_total = jnp.dot(sketch.T, sketch, precision=highest)
    lower = jnp.linalg.cholesky(gram_total)
    ortho = jax.scipy.linalg.solve_triangular(lower, sketch.T, lower=True).T
    factor = jnp.dot(ortho.T, sample, precision=highest)
    basis = ortho * jnp.sqrt(jnp.float32(M))
    return (basis, factor)
```

```python
import functools

import jax
import jax.numpy as jnp
from jax import lax
from jax.experimental import pallas as pl
from jax.experimental.pallas import tpu as pltpu
from jax.sharding import PartitionSpec as P

MESH = pl.DeviceIdType.MESH
f32, bf16 = jnp.float32, jnp.bfloat16
NX, NY, NZ = 4, 4, 16
RANK, D, ROWS = 256, 1024, 1024
COLS = D // 128
PLANE = [(a, b) for a in range(NX) for b in range(NY) if a or b]


def split(v):
    hi = v.astype(bf16)
    return hi, (v - hi.astype(f32)).astype(bf16)


def mm(a, b, dims):
    def dot(u, v):
        return lax.dot_general(u, v, (dims, ((), ())), preferred_element_type=f32)

    (ah, al), (bh, bl) = a, b
    return dot(ah, bh) + (dot(ah, bl) + dot(al, bh))


def reduce_kernel(s_hbm, t_ref, sk_ref, o_ref, s_ref, sh, sl, skt, w, core_in, s0, r1, zs, rz, zt, za, out, load,
                  ssc, rsc, ss1, rs1, ssz, rsz, sgz, rgz, sg1, rg1, sgc, rgc):
    r = lax.axis_index("rows")
    g = lax.axis_index("grp")
    x, y, z, c = lax.div(r, NZ), lax.div(g, 2), lax.rem(r, NZ), lax.rem(g, 2)
    o = 1 - c

    def at(dx, dy, dz):
        return (lax.rem(x + dx, NX) * NZ + lax.rem(z + dz, NZ), lax.rem(y + dy, NY) * 2 + c)

    partner = (r, y * 2 + o)

    def copy(src, dst, ss, rs, dev):
        return pltpu.make_async_remote_copy(src_ref=src, dst_ref=dst, send_sem=ss, recv_sem=rs, device_id=dev, device_id_type=MESH)

    def rows(a, n):
        return pl.ds(pl.multiple_of(a, 8), n)

    n = ROWS // 4
    loads = [pltpu.make_async_copy(s_hbm.at[pl.ds(i * n, n)], s_ref.at[pl.ds(i * n, n)], load.at[i]) for i in range(4)]
    for k in loads:
        k.start()
    barrier = pltpu.get_barrier_semaphore()

    def greet(dev):
        pl.semaphore_signal(barrier, inc=1, device_id=dev, device_id_type=MESH)

    greet(partner)
    for dx, dy in PLANE:
        greet(at(dx, dy, 0))

    def greet_z(d, _):
        greet(at(0, 0, d))
        return 0

    lax.fori_loop(1, NZ, greet_z, 0)

    t = split(t_ref[...].T)
    for i in range(4):
        loads[i].wait()
        at_i = pl.ds(i * n, n)
        s = split(s_ref[at_i, :])
        sh[at_i, :], sl[at_i, :] = s
        skt[:, at_i] = mm(t, s, ((1,), (1,)))
    sk = split(skt[...])

    core = []
    for q in range(4):
        lanes = pl.ds(256 * q, 256)
        d = mm(sk, (sh[:, lanes], sl[:, lanes]), ((1,), (0,)))
        w[2 * q] = d[:, :128]
        w[2 * q + 1] = d[:, 128:]
        if q == 0:
            pl.semaphore_wait(barrier, 1 + len(PLANE) + NZ - 1)
        pair = pl.ds(2 * q, 2)
        k = copy(w.at[pair, rows(128 * o, 128)], core_in.at[pair], ssc.at[q], rsc.at[q], partner)
        k.start()
        core.append(k)
    for q in range(4):
        core[q].wait_recv()
        pair = pl.ds(2 * q, 2)
        s0[pair] = w[pair, rows(128 * c, 128), :] + core_in[pair]

    plane = []
    for i, (dx, dy) in enumerate(PLANE):
        q = lax.rem(x + dx, NX) * NY + lax.rem(y + dy, NY)
        k = copy(s0.at[:, rows(8 * q, 8)], r1.at[i], ss1.at[i], rs1.at[i], at(dx, dy, 0))
        k.start()
        plane.append(k)
    sk_ref[...] = skt[...].T
    own = 8 * (x * NY + y)
    for k in plane:
        k.wait_recv()
    v = s0[:, rows(own, 8), :]
    for i in range(len(PLANE)):
        v = v + r1[i]
    for j in range(COLS):
        zs[2 * j] = v[j, 0:4]
        zs[2 * j + 1] = v[j, 4:8]

    def z_copy(d):
        return copy(zs.at[lax.rem(z + d, NZ)], rz.at[d], ssz.at[d], rsz.at[d], at(0, 0, d))

    def each_z(step):
        def body(d, _):
            step(d)
            return 0

        lax.fori_loop(1, NZ, body, 0)

    each_z(lambda d: z_copy(d).start())
    each_z(lambda d: z_copy(d).wait_recv())
    v = zs[z]
    for d in range(1, NZ):
        v = v + rz[d]
    zt[...] = v
    za[z] = v

    def g_copy(d):
        return copy(zt, za.at[z], sgz.at[d], rgz.at[d], at(0, 0, d))

    each_z(lambda d: g_copy(d).start())
    each_z(lambda d: g_copy(d).wait_recv())
    mine = 128 * c + own
    for j in range(COLS):
        out[j, rows(mine, 8), :] = jnp.concatenate([za[2 * j], za[2 * j + 1]], axis=0)

    def back(i, dx, dy):
        ref = out.at[:, rows(mine, 8)]
        return copy(ref, ref, sg1.at[i], rg1.at[i], at(dx, dy, 0))

    gather = [back(i, dx, dy) for i, (dx, dy) in enumerate(PLANE)]
    for k in gather:
        k.start()
    for k in gather:
        k.wait_recv()
    ref = out.at[:, rows(128 * c, 128)]
    last = copy(ref, ref, sgc, rgc, partner)
    last.start()
    last.wait_recv()
    for k in core + plane + gather + [last]:
        k.wait_send()
    each_z(lambda d: z_copy(d).wait_send())
    each_z(lambda d: g_copy(d).wait_send())
    o_ref[...] = out[...]


def sketch_and_sum(sample, test_matrix):
    V, S = pltpu.VMEM, pltpu.SemaphoreType.DMA
    n = len(PLANE)
    return pl.pallas_call(
        reduce_kernel,
        out_shape=(jax.ShapeDtypeStruct((ROWS, RANK), f32), jax.ShapeDtypeStruct((COLS, RANK, 128), f32)),
        in_specs=[pl.BlockSpec(memory_space=pl.ANY), pl.BlockSpec(memory_space=pltpu.VMEM)],
        out_specs=(pl.BlockSpec(memory_space=pltpu.VMEM),) * 2,
        scratch_shapes=[
            V((ROWS, D), f32), V((ROWS, D), bf16), V((ROWS, D), bf16), V((RANK, ROWS), f32), V((COLS, RANK, 128), f32),
            V((COLS, 128, 128), f32), V((COLS, 128, 128), f32), V((n, COLS, 8, 128), f32), V((NZ, 4, 128), f32),
            V((NZ, 4, 128), f32), V((4, 128), f32), V((NZ, 4, 128), f32), V((COLS, RANK, 128), f32), S((4,)),
            S((4,)), S((4,)), S((n,)), S((n,)), S((NZ,)), S((NZ,)), S((NZ,)), S((NZ,)), S((n,)), S((n,)), S, S,
        ],
        compiler_params=pltpu.CompilerParams(collective_id=0, has_side_effects=True, vmem_limit_bytes=56 << 20),
    )(sample, test_matrix)


def inverse_factor(gram, x_ref, group=8):
    n = RANK
    lane = lax.broadcasted_iota(jnp.int32, (8, n), 1)
    sub = lax.broadcasted_iota(jnp.int32, (8, n), 0)
    sub1 = lax.broadcasted_iota(jnp.int32, (8, 128), 0)
    blocks = n // 8

    def wide(v):
        return jnp.concatenate([v] * (n // 128), axis=1)

    rows = [gram[8 * i : 8 * i + 8, :] for i in range(blocks)]
    for top in range(0, blocks, group):
        end = top + group
        for k in range(top, end):
            own = (lane >= 8 * k) & (lane < 8 * k + 8)
            cols = {}
            for i in range(k, end):
                cols[i] = [jnp.broadcast_to(rows[i][:, 8 * k + s : 8 * k + s + 1], (8, 128)) for s in range(8)]
                rows[i] = jnp.where(own, (lane - 8 * k == sub).astype(f32) if i == k else 0.0, rows[i])
            scale = jnp.zeros((8, 128), f32)
            for s in range(8):
                pivot = jnp.broadcast_to(cols[k][s][s : s + 1, :], (8, 128))
                inv = 1.0 / pivot
                row = jnp.broadcast_to(rows[k][s : s + 1, :], (8, n))
                heads = [jnp.broadcast_to(cols[k][u][s : s + 1, :], (8, 128)) for u in range(s + 1, 8)]
                for i in range(k, end):
                    m = cols[i][s] * inv
                    if i == k:
                        m = jnp.where(sub1 > s, m, 0.0)
                    for u in range(s + 1, 8):
                        cols[i][u] = cols[i][u] - m * heads[u - s - 1]
                    rows[i] = rows[i] - wide(m) * row
                scale = jnp.where(sub1 == s, lax.rsqrt(pivot), scale)
            rows[k] = jnp.where((lane < 8 * k + 8) | (lane >= 8 * end), rows[k] * wide(scale), 0.0)
            x_ref[8 * k : 8 * k + 8, :] = jnp.where(lane < 8 * k + 8, rows[k], 0.0)
        if end < blocks:
            v = jnp.concatenate(rows[top:end], axis=0)
            d = lax.dot_general(
                v[:, 8 * end :], v, (((0,), (0,)), ((), ())), precision=lax.Precision.HIGHEST, preferred_element_type=f32
            )
            done = (lane >= 8 * top) & (lane < 8 * end)
            for i in range(end, blocks):
                rows[i] = jnp.where(done, 0.0, rows[i]) - d[8 * (i - end) : 8 * (i - end) + 8, :]


def finish_kernel(sk_ref, w_ref, t_ref, b_ref, f_ref, x_ref, scale):
    high = lax.Precision.HIGHEST
    gram = jnp.zeros((RANK, RANK), f32)
    for j in range(0, COLS, 2):
        pair = jnp.concatenate([w_ref[j], w_ref[j + 1]], axis=1)
        gram = gram + jnp.dot(pair, t_ref[128 * j : 128 * j + 256, :], precision=high, preferred_element_type=f32)
    inverse_factor(gram, x_ref)
    x = split(x_ref[...])
    for i in range(4):
        at_i = pl.ds(256 * i, 256)
        b_ref[at_i, :] = mm(split(sk_ref[at_i, :]), x, ((1,), (1,))) * scale
        pair = jnp.concatenate([w_ref[2 * i], w_ref[2 * i + 1]], axis=1)
        f_ref[:, at_i] = mm(x, split(pair), ((1,), (0,)))


def finish(sk, total, test_matrix, scale):
    spec = pl.BlockSpec(memory_space=pltpu.VMEM)
    return pl.pallas_call(
        functools.partial(finish_kernel, scale=scale),
        out_shape=(jax.ShapeDtypeStruct((ROWS, RANK), f32), jax.ShapeDtypeStruct((RANK, D), f32)),
        in_specs=[spec] * 3,
        out_specs=(spec,) * 2,
        scratch_shapes=[pltpu.VMEM((RANK, RANK), f32)],
        compiler_params=pltpu.CompilerParams(vmem_limit_bytes=40 << 20),
    )(sk, total, test_matrix)


def body(sample, test_matrix):
    devices = lax.axis_size("rows") * lax.axis_size("grp")
    sk, total = sketch_and_sum(sample, test_matrix)
    return finish(sk, total, test_matrix, float((ROWS * devices) ** 0.5))


def solution(mesh):
    placed = (P(("rows", "grp"), None), P())
    return jax.shard_map(
        body, mesh=mesh, in_specs=placed, out_specs=(P(("rows", "grp"), None), P()), check_vma=False
    )
```

```python
import functools

import jax
import jax.numpy as jnp
from jax import lax
from jax.experimental import pallas as pl
from jax.experimental.pallas import tpu as pltpu
from jax.sharding import PartitionSpec as P

MESH = pl.DeviceIdType.MESH
f32, bf16 = jnp.float32, jnp.bfloat16
NX, NY, NZ = 4, 4, 16
RANK, D, ROWS = 256, 1024, 1024
COLS = D // 128
PLANE = sorted(((a, b) for a in range(NX) for b in range(NY) if a or b), key=lambda v: -min(v[0], NX - v[0]) - min(v[1], NY - v[1]))
RING = sorted(range(1, NZ), key=lambda d: -min(d, NZ - d))
PARTS = 2
PB = COLS // PARTS
PIECE = 8 * PB // NZ


def split(v):
    hi = v.astype(bf16)
    return hi, (v - hi.astype(f32)).astype(bf16)


def mm(a, b, dims):
    def dot(u, v):
        return lax.dot_general(u, v, (dims, ((), ())), preferred_element_type=f32)

    (ah, al), (bh, bl) = a, b
    return dot(ah, bh) + (dot(ah, bl) + dot(al, bh))


def reduce_kernel(s_hbm, t_hbm, sk_ref, o_ref, x_ref, s_ref, t_ref, sh, sl, skt, w, core_in, s0, r1, zs, rz, zt, za, out,
                  gl, gcore_in, gs0, gr1, gz, go, load, ssc, rsc, ssp, rsp, ssz, rsz):
    r = lax.axis_index("rows")
    g = lax.axis_index("grp")
    x, y, z, c = lax.div(r, NZ), lax.div(g, 2), lax.rem(r, NZ), lax.rem(g, 2)
    o = 1 - c

    def at(dx, dy, dz):
        return (lax.rem(x + dx, NX) * NZ + lax.rem(z + dz, NZ), lax.rem(y + dy, NY) * 2 + c)

    partner = (r, y * 2 + o)
    started = []

    def rows(a, n):
        return pl.ds(pl.multiple_of(a, 8), n)

    def send(src, dst, ss, rs, dev):
        k = pltpu.make_async_remote_copy(src_ref=src, dst_ref=dst, send_sem=ss, recv_sem=rs, device_id=dev, device_id_type=MESH)
        k.start()
        started.append(k)
        return k

    def arrive(copies):
        for k in copies:
            k.wait_recv()

    def core_send(phase, src, dst):
        return send(src, dst, ssc.at[phase], rsc.at[phase], partner)

    def plane_send(phase, src, dst):
        copies = []
        for i, (dx, dy) in enumerate(PLANE):
            q = lax.rem(x + dx, NX) * NY + lax.rem(y + dy, NY)
            copies.append(send(src(q), dst(i), ssp.at[phase, i], rsp.at[phase, i], at(dx, dy, 0)))
        return copies

    def z_send(phase, src, dst):
        return [send(src(lax.rem(z + d, NZ)), dst(d), ssz.at[phase, d], rsz.at[phase, d], at(0, 0, d)) for d in RING]

    n = ROWS // 4
    t_load = pltpu.make_async_copy(t_hbm, t_ref, load.at[4])
    t_load.start()
    loads = [pltpu.make_async_copy(s_hbm.at[pl.ds(i * n, n)], s_ref.at[pl.ds(i * n, n)], load.at[i]) for i in range(4)]
    for k in loads:
        k.start()
    barrier = pltpu.get_barrier_semaphore()

    def greet(dev):
        pl.semaphore_signal(barrier, inc=1, device_id=dev, device_id_type=MESH)

    for d in RING:
        greet(at(0, 0, d))
    for dx, dy in PLANE:
        greet(at(dx, dy, 0))
    greet(partner)

    t_load.wait()
    t = split(t_ref[...])
    gram = jnp.zeros((RANK, RANK), f32)
    for i in range(4):
        loads[i].wait()
        at_i = pl.ds(i * n, n)
        s = split(s_ref[at_i, :])
        sh[at_i, :], sl[at_i, :] = s
        part = mm(s, t, ((1,), (0,)))
        turned = part.T
        sk_ref[at_i, :] = part
        skt[:, at_i] = turned
        gram = gram + mm(split(turned), split(part), ((1,), (0,)))
    gl[0] = gram[:, :128]
    gl[1] = gram[:, 128:]
    pl.semaphore_wait(barrier, 1 + len(PLANE) + len(RING))
    mine, theirs = rows(128 * c, 128), rows(128 * o, 128)
    g_core = core_send(0, gl.at[:, theirs], gcore_in)

    sk = split(skt[...])
    w_core = []

    def multiply(q):
        lanes = pl.ds(256 * q, 256)
        d = mm(sk, (sh[:, lanes], sl[:, lanes]), ((1,), (0,)))
        w[2 * q] = d[:, :128]
        w[2 * q + 1] = d[:, 128:]
        pair = pl.ds(2 * q, 2)
        w_core.append(core_send(1 + q, w.at[pair, theirs], core_in.at[pair]))

    multiply(0)
    multiply(1)
    arrive([g_core])
    gs0[...] = gl[:, mine, :] + gcore_in[...]
    g_plane = plane_send(0, lambda q: gs0.at[:, rows(8 * q, 8)], lambda i: gr1.at[i])
    multiply(2)
    multiply(3)

    own = rows(8 * (x * NY + y), 8)
    w_plane = []
    for h in range(PARTS):
        at_h = pl.ds(PB * h, PB)
        arrive(w_core[h * 4 // PARTS : (h + 1) * 4 // PARTS])
        s0[at_h] = w[at_h, mine, :] + core_in[at_h]
        w_plane.append(plane_send(1 + h, lambda q: s0.at[at_h, rows(8 * q, 8)], lambda i: r1.at[h, i]))

    arrive(g_plane)
    v = gs0[:, own, :]
    for i in range(len(PLANE)):
        v = v + gr1[i]
    gz[z] = v
    g_z = z_send(0, lambda q: gz.at[z], lambda d: gz.at[z])

    w_z = []
    for h in range(PARTS):
        arrive(w_plane[h])
        v = s0[pl.ds(PB * h, PB), own, :]
        for i in range(len(PLANE)):
            v = v + r1[h, i]
        for j in range(PB):
            for p in range(8 // PIECE):
                zs[h, j * (8 // PIECE) + p] = v[j, p * PIECE : (p + 1) * PIECE]
        w_z.append(z_send(1 + h, lambda q: zs.at[h, q], lambda d: rz.at[h, d]))

    arrive(g_z)
    v = gz[0]
    for d in range(1, NZ):
        v = v + gz[d]
    place = rows(128 * c + 8 * (x * NY + y), 8)
    go[:, place, :] = v
    g_back = plane_send(1 + PARTS, lambda q: go.at[:, place], lambda i: go.at[:, place])

    w_all = []
    for h in range(PARTS):
        arrive(w_z[h])
        v = zs[h, z]
        for d in RING:
            v = v + rz[h, d]
        zt[h] = v
        za[h, z] = v
        w_all.append(z_send(1 + PARTS + h, lambda q: zt.at[h], lambda d: za.at[h, z]))

    arrive(g_back)
    arrive([core_send(5, go.at[:, mine], go.at[:, mine])])

    w_back = []

    def between(i):
        if i >= PARTS:
            return
        arrive(w_all[i])
        for j in range(PB):
            k = 8 // PIECE
            out[PB * i + j, place, :] = jnp.concatenate([za[i, j * k + p] for p in range(k)], axis=0)
        ref = out.at[pl.ds(PB * i, PB), place]
        w_back.append(plane_send(2 + PARTS + i, lambda q: ref, lambda d: ref))

    blocks = [jnp.concatenate([go[0, 8 * i : 8 * i + 8, :], go[1, 8 * i : 8 * i + 8, :]], axis=1) for i in range(RANK // 8)]
    inverse_factor(blocks, x_ref, between)

    last = []
    for h in range(PARTS):
        arrive(w_back[h])
        ref = out.at[pl.ds(PB * h, PB), mine]
        last.append(core_send(6 + h, ref, ref))
    arrive(last)
    for k in started:
        k.wait_send()
    o_ref[...] = out[...]


def sketch_and_sum(sample, test_matrix):
    V, S = pltpu.VMEM, pltpu.SemaphoreType.DMA
    n = len(PLANE)
    spec = pl.BlockSpec(memory_space=pltpu.VMEM)
    return pl.pallas_call(
        reduce_kernel,
        out_shape=(
            jax.ShapeDtypeStruct((ROWS, RANK), f32),
            jax.ShapeDtypeStruct((COLS, RANK, 128), f32),
            jax.ShapeDtypeStruct((RANK, RANK), f32),
        ),
        in_specs=[pl.BlockSpec(memory_space=pl.ANY)] * 2,
        out_specs=(spec,) * 3,
        scratch_shapes=[
            V((ROWS, D), f32), V((D, RANK), f32), V((ROWS, D), bf16), V((ROWS, D), bf16), V((RANK, ROWS), f32),
            V((COLS, RANK, 128), f32), V((COLS, 128, 128), f32), V((COLS, 128, 128), f32), V((PARTS, n, PB, 8, 128), f32),
            V((PARTS, NZ, PIECE, 128), f32), V((PARTS, NZ, PIECE, 128), f32), V((PARTS, PIECE, 128), f32),
            V((PARTS, NZ, PIECE, 128), f32), V((COLS, RANK, 128), f32),
            V((2, RANK, 128), f32), V((2, 128, 128), f32), V((2, 128, 128), f32), V((n, 2, 8, 128), f32),
            V((NZ, 2, 8, 128), f32), V((2, RANK, 128), f32),
            S((5,)), S((6 + PARTS,)), S((6 + PARTS,)), S((2 + 2 * PARTS, n)), S((2 + 2 * PARTS, n)),
            S((1 + 2 * PARTS, NZ)), S((1 + 2 * PARTS, NZ)),
        ],
        compiler_params=pltpu.CompilerParams(collective_id=0, has_side_effects=True, vmem_limit_bytes=60 << 20),
    )(sample, test_matrix)


def inverse_factor(rows, x_ref, between, group=8):
    n = RANK
    lane = lax.broadcasted_iota(jnp.int32, (8, n), 1)
    sub = lax.broadcasted_iota(jnp.int32, (8, n), 0)
    sub1 = lax.broadcasted_iota(jnp.int32, (8, 128), 0)
    blocks = n // 8

    def wide(v):
        return jnp.concatenate([v] * (n // 128), axis=1)

    for top in range(0, blocks, group):
        end = top + group
        for k in range(top, end):
            own = (lane >= 8 * k) & (lane < 8 * k + 8)
            cols = {}
            for i in range(k, end):
                cols[i] = [jnp.broadcast_to(rows[i][:, 8 * k + s : 8 * k + s + 1], (8, 128)) for s in range(8)]
                rows[i] = jnp.where(own, (lane - 8 * k == sub).astype(f32) if i == k else 0.0, rows[i])
            scale = jnp.zeros((8, 128), f32)
            for s in range(8):
                pivot = jnp.broadcast_to(cols[k][s][s : s + 1, :], (8, 128))
                inv = 1.0 / pivot
                row = jnp.broadcast_to(rows[k][s : s + 1, :], (8, n))
                heads = [jnp.broadcast_to(cols[k][u][s : s + 1, :], (8, 128)) for u in range(s + 1, 8)]
                for i in range(k, end):
                    m = cols[i][s] * inv
                    if i == k:
                        m = jnp.where(sub1 > s, m, 0.0)
                    for u in range(s + 1, 8):
                        cols[i][u] = cols[i][u] - m * heads[u - s - 1]
                    rows[i] = rows[i] - wide(m) * row
                scale = jnp.where(sub1 == s, lax.rsqrt(pivot), scale)
            rows[k] = jnp.where((lane < 8 * k + 8) | (lane >= 8 * end), rows[k] * wide(scale), 0.0)
            x_ref[8 * k : 8 * k + 8, :] = jnp.where(lane < 8 * k + 8, rows[k], 0.0)
        if end < blocks:
            v = jnp.concatenate(rows[top:end], axis=0)
            d = lax.dot_general(
                v[:, 8 * end :], v, (((0,), (0,)), ((), ())), precision=lax.Precision.HIGHEST, preferred_element_type=f32
            )
            done = (lane >= 8 * top) & (lane < 8 * end)
            for i in range(end, blocks):
                rows[i] = jnp.where(done, 0.0, rows[i]) - d[8 * (i - end) : 8 * (i - end) + 8, :]
        between(top // group)


def finish_kernel(sk_hbm, w_hbm, x_hbm, b_hbm, f_hbm, sk, w, x, b, f, load, store, scale):
    n = ROWS // 4

    def take(src, dst, i):
        k = pltpu.make_async_copy(src, dst, load.at[i])
        k.start()
        return k

    x_load = take(x_hbm, x, 8)
    w_load = [take(w_hbm.at[pl.ds(2 * i, 2)], w.at[pl.ds(2 * i, 2)], i) for i in range(4)]
    sk_load = [take(sk_hbm.at[pl.ds(n * i, n)], sk.at[pl.ds(n * i, n)], 4 + i) for i in range(4)]
    x_load.wait()
    inv = split(x[...])
    stores = []

    def give(src, dst, i):
        k = pltpu.make_async_copy(src, dst, store.at[i])
        k.start()
        stores.append(k)

    for i in range(4):
        lanes = pl.ds(256 * i, 256)
        w_load[i].wait()
        pair = jnp.concatenate([w[2 * i], w[2 * i + 1]], axis=1)
        f[:, lanes] = mm(inv, split(pair), ((1,), (0,)))
        give(f.at[:, lanes], f_hbm.at[:, lanes], i)
    turned = split(x[...].T)
    for i in range(4):
        at_i = pl.ds(n * i, n)
        sk_load[i].wait()
        b[at_i, :] = mm(split(sk[at_i, :]), turned, ((1,), (0,))) * scale
        give(b.at[at_i], b_hbm.at[at_i], 4 + i)
    for k in stores:
        k.wait()


def finish(sk, total, inverse, scale):
    V, S = pltpu.VMEM, pltpu.SemaphoreType.DMA
    spec = pl.BlockSpec(memory_space=pl.ANY)
    return pl.pallas_call(
        functools.partial(finish_kernel, scale=scale),
        out_shape=(jax.ShapeDtypeStruct((ROWS, RANK), f32), jax.ShapeDtypeStruct((RANK, D), f32)),
        in_specs=[spec] * 3,
        out_specs=(spec,) * 2,
        scratch_shapes=[
            V((ROWS, RANK), f32), V((COLS, RANK, 128), f32), V((RANK, RANK), f32), V((ROWS, RANK), f32), V((RANK, D), f32),
            S((9,)), S((8,)),
        ],
        compiler_params=pltpu.CompilerParams(vmem_limit_bytes=60 << 20),
    )(sk, total, inverse)


def body(sample, test_matrix):
    devices = lax.axis_size("rows") * lax.axis_size("grp")
    sk, total, inverse = sketch_and_sum(sample, test_matrix)
    return finish(sk, total, inverse, float((ROWS * devices) ** 0.5))


def solution(mesh):
    placed = (P(("rows", "grp"), None), P())
    return jax.shard_map(
        body, mesh=mesh, in_specs=placed, out_specs=(P(("rows", "grp"), None), P()), check_vma=False
    )
```

```python
import functools

import jax
import jax.numpy as jnp
from jax import lax
from jax.experimental import pallas as pl
from jax.experimental.pallas import tpu as pltpu
from jax.sharding import PartitionSpec as P

MESH = pl.DeviceIdType.MESH
f32, bf16 = jnp.float32, jnp.bfloat16
NX, NY, NZ = 4, 4, 16
RANK, D, ROWS = 256, 1024, 1024
COLS = D // 128
PLANE = sorted(((a, b) for a in range(NX) for b in range(NY) if a or b), key=lambda v: -min(v[0], NX - v[0]) - min(v[1], NY - v[1]))
RING = sorted(range(1, NZ), key=lambda d: -min(d, NZ - d))
PARTS = 2
PB = COLS // PARTS
PIECE = 8 * PB // NZ


def split(v):
    hi = v.astype(bf16)
    return hi, (v - hi.astype(f32)).astype(bf16)


def mm(a, b, dims):
    def dot(u, v):
        return lax.dot_general(u, v, (dims, ((), ())), preferred_element_type=f32)

    (ah, al), (bh, bl) = a, b
    return dot(ah, bh) + (dot(ah, bl) + dot(al, bh))


def reduce_kernel(s_hbm, t_hbm, b_hbm, o_hbm, x_hbm, sk_ref, x_ref, b, s_ref, t_ref, sh, sl, skt, w, core_in, s0, r1, zs, rz, zt, za, out,
                  gl, gcore_in, gs0, gr1, gz, go, load, store, ssc, rsc, ssp, rsp, ssz, rsz, scale):
    r = lax.axis_index("rows")
    g = lax.axis_index("grp")
    x, y, z, c = lax.div(r, NZ), lax.div(g, 2), lax.rem(r, NZ), lax.rem(g, 2)
    o = 1 - c

    def at(dx, dy, dz):
        return (lax.rem(x + dx, NX) * NZ + lax.rem(z + dz, NZ), lax.rem(y + dy, NY) * 2 + c)

    partner = (r, y * 2 + o)
    started, kept = [], []

    def rows(a, n):
        return pl.ds(pl.multiple_of(a, 8), n)

    def send(src, dst, ss, rs, dev):
        k = pltpu.make_async_remote_copy(src_ref=src, dst_ref=dst, send_sem=ss, recv_sem=rs, device_id=dev, device_id_type=MESH)
        k.start()
        started.append(k)
        return k

    def arrive(copies):
        for k in copies:
            k.wait_recv()

    def core_send(phase, src, dst):
        return send(src, dst, ssc.at[phase], rsc.at[phase], partner)

    def plane_send(phase, src, dst):
        copies = []
        for i, (dx, dy) in enumerate(PLANE):
            q = lax.rem(x + dx, NX) * NY + lax.rem(y + dy, NY)
            copies.append(send(src(q), dst(i), ssp.at[phase, i], rsp.at[phase, i], at(dx, dy, 0)))
        return copies

    def z_send(phase, src, dst):
        return [send(src(lax.rem(z + d, NZ)), dst(d), ssz.at[phase, d], rsz.at[phase, d], at(0, 0, d)) for d in RING]

    def keep(src, dst, i):
        k = pltpu.make_async_copy(src, dst, store.at[i])
        k.start()
        kept.append(k)

    n = ROWS // 2
    t_load = pltpu.make_async_copy(t_hbm, t_ref, load.at[2])
    t_load.start()
    loads = [pltpu.make_async_copy(s_hbm.at[pl.ds(i * n, n)], s_ref.at[pl.ds(i * n, n)], load.at[i]) for i in range(2)]
    for k in loads:
        k.start()
    barrier = pltpu.get_barrier_semaphore()

    def greet(dev):
        pl.semaphore_signal(barrier, inc=1, device_id=dev, device_id_type=MESH)

    for d in RING:
        greet(at(0, 0, d))
    for dx, dy in PLANE:
        greet(at(dx, dy, 0))
    greet(partner)

    t_load.wait()
    t = split(t_ref[...].T)
    for i in range(2):
        loads[i].wait()
        at_i = pl.ds(i * n, n)
        s = split(s_ref[at_i, :])
        sh[at_i, :], sl[at_i, :] = s
        skt[:, at_i] = mm(t, s, ((1,), (1,)))

    sk = split(skt[...])
    for q in range(4):
        lanes = pl.ds(256 * q, 256)
        d = mm(sk, (sh[:, lanes], sl[:, lanes]), ((1,), (0,)))
        w[2 * q] = d[:, :128]
        w[2 * q + 1] = d[:, 128:]
    whole = jnp.concatenate([w[j] for j in range(COLS)], axis=1)
    gram = mm(split(whole), split(t_ref[...]), ((1,), (0,)))
    gl[0] = gram[:, :128]
    gl[1] = gram[:, 128:]

    mine, theirs = rows(128 * c, 128), rows(128 * o, 128)
    pl.semaphore_wait(barrier, 1 + len(PLANE) + len(RING))
    g_core = core_send(0, gl.at[:, theirs], gcore_in)
    w_core = []
    for h in range(PARTS):
        at_h = pl.ds(PB * h, PB)
        w_core.append(core_send(1 + h, w.at[at_h, theirs], core_in.at[at_h]))

    own = rows(8 * (x * NY + y), 8)
    arrive([g_core])
    gs0[...] = gl[:, mine, :] + gcore_in[...]
    g_plane = plane_send(0, lambda q: gs0.at[:, rows(8 * q, 8)], lambda i: gr1.at[i])
    w_plane = []
    for h in range(PARTS):
        at_h = pl.ds(PB * h, PB)
        arrive(w_core[h : h + 1])
        s0[at_h] = w[at_h, mine, :] + core_in[at_h]
        w_plane.append(plane_send(1 + h, lambda q: s0.at[at_h, rows(8 * q, 8)], lambda i: r1.at[h, i]))
    sk_ref[...] = skt[...].T

    arrive(g_plane)
    v = gs0[:, own, :]
    for i in range(len(PLANE)):
        v = v + gr1[i]
    gz[z] = v
    g_z = z_send(0, lambda q: gz.at[z], lambda d: gz.at[z])

    w_z = []
    for h in range(PARTS):
        arrive(w_plane[h])
        v = s0[pl.ds(PB * h, PB), own, :]
        for i in range(len(PLANE)):
            v = v + r1[h, i]
        for j in range(PB):
            for p in range(8 // PIECE):
                zs[h, j * (8 // PIECE) + p] = v[j, p * PIECE : (p + 1) * PIECE]
        w_z.append(z_send(1 + h, lambda q: zs.at[h, q], lambda d: rz.at[h, d]))

    arrive(g_z)
    v = gz[0]
    for d in range(1, NZ):
        v = v + gz[d]
    place = rows(128 * c + 8 * (x * NY + y), 8)
    go[:, place, :] = v
    g_back = plane_send(1 + PARTS, lambda q: go.at[:, place], lambda i: go.at[:, place])

    w_all = []
    for h in range(PARTS):
        arrive(w_z[h])
        v = zs[h, z]
        for d in RING:
            v = v + rz[h, d]
        zt[h] = v
        za[h, z] = v
        w_all.append(z_send(1 + PARTS + h, lambda q: zt.at[h], lambda d: za.at[h, z]))

    arrive(g_back)
    arrive([core_send(1 + PARTS, go.at[:, mine], go.at[:, mine])])

    w_back = []

    def between(i):
        if i != 1:
            return
        for h in range(PARTS):
            arrive(w_all[h])
            for j in range(PB):
                k = 8 // PIECE
                out[PB * h + j, place, :] = jnp.concatenate([za[h, j * k + p] for p in range(k)], axis=0)
            ref = out.at[pl.ds(PB * h, PB), place]
            w_back.append(plane_send(2 + PARTS + h, lambda q: ref, lambda d: ref))

    blocks = [jnp.concatenate([go[0, 8 * i : 8 * i + 8, :], go[1, 8 * i : 8 * i + 8, :]], axis=1) for i in range(RANK // 8)]
    inverse_factor(blocks, x_ref, between)

    keep(x_ref, x_hbm, 2 * PARTS)
    turned = split(x_ref[...].T)
    n = ROWS // 4
    for i in range(4):
        at_i = pl.ds(n * i, n)
        b[at_i, :] = mm(split(sk_ref[at_i, :]), turned, ((1,), (0,))) * scale
        keep(b.at[at_i], b_hbm.at[at_i], 2 * PARTS + 1 + i)
    last = []
    for h in range(PARTS):
        arrive(w_back[h])
        ref = out.at[pl.ds(PB * h, PB), mine]
        last.append(core_send(2 + PARTS + h, ref, ref))
        keep(ref, o_hbm.at[pl.ds(PB * h, PB), mine], h)
    for h in range(PARTS):
        arrive(last[h : h + 1])
        keep(out.at[pl.ds(PB * h, PB), theirs], o_hbm.at[pl.ds(PB * h, PB), theirs], PARTS + h)
    for k in started:
        k.wait_send()
    for k in kept:
        k.wait()


def sketch_and_sum(sample, test_matrix, scale):
    V, S = pltpu.VMEM, pltpu.SemaphoreType.DMA
    n = len(PLANE)
    spec = pl.BlockSpec(memory_space=pl.ANY)
    return pl.pallas_call(
        functools.partial(reduce_kernel, scale=scale),
        out_shape=(
            jax.ShapeDtypeStruct((ROWS, RANK), f32),
            jax.ShapeDtypeStruct((COLS, RANK, 128), f32),
            jax.ShapeDtypeStruct((RANK, RANK), f32),
        ),
        in_specs=[spec] * 2,
        out_specs=(spec,) * 3,
        scratch_shapes=[
            V((ROWS, RANK), f32), V((RANK, RANK), f32), V((ROWS, RANK), f32),
            V((ROWS, D), f32), V((D, RANK), f32), V((ROWS, D), bf16), V((ROWS, D), bf16), V((RANK, ROWS), f32),
            V((COLS, RANK, 128), f32), V((COLS, 128, 128), f32), V((COLS, 128, 128), f32), V((PARTS, n, PB, 8, 128), f32),
            V((PARTS, NZ, PIECE, 128), f32), V((PARTS, NZ, PIECE, 128), f32), V((PARTS, PIECE, 128), f32),
            V((PARTS, NZ, PIECE, 128), f32), V((COLS, RANK, 128), f32),
            V((2, RANK, 128), f32), V((2, 128, 128), f32), V((2, 128, 128), f32), V((n, 2, 8, 128), f32),
            V((NZ, 2, 8, 128), f32), V((2, RANK, 128), f32),
            S((3,)), S((2 * PARTS + 5,)), S((2 + 2 * PARTS,)), S((2 + 2 * PARTS,)), S((2 + 2 * PARTS, n)), S((2 + 2 * PARTS, n)),
            S((1 + 2 * PARTS, NZ)), S((1 + 2 * PARTS, NZ)),
        ],
        compiler_params=pltpu.CompilerParams(collective_id=0, has_side_effects=True, vmem_limit_bytes=60 << 20),
    )(sample, test_matrix)


def inverse_factor(rows, x_ref, between, group=8):
    n = RANK
    lane = lax.broadcasted_iota(jnp.int32, (8, n), 1)
    sub = lax.broadcasted_iota(jnp.int32, (8, n), 0)
    sub1 = lax.broadcasted_iota(jnp.int32, (8, 128), 0)
    blocks = n // 8

    def wide(v):
        return jnp.concatenate([v] * (n // 128), axis=1)

    for top in range(0, blocks, group):
        end = top + group
        for k in range(top, end):
            own = (lane >= 8 * k) & (lane < 8 * k + 8)
            cols = {}
            for i in range(k, end):
                cols[i] = [jnp.broadcast_to(rows[i][:, 8 * k + s : 8 * k + s + 1], (8, 128)) for s in range(8)]
                rows[i] = jnp.where(own, (lane - 8 * k == sub).astype(f32) if i == k else 0.0, rows[i])
            scale = jnp.zeros((8, 128), f32)
            for s in range(8):
                pivot = jnp.broadcast_to(cols[k][s][s : s + 1, :], (8, 128))
                inv = 1.0 / pivot
                row = jnp.broadcast_to(rows[k][s : s + 1, :], (8, n))
                heads = [jnp.broadcast_to(cols[k][u][s : s + 1, :], (8, 128)) for u in range(s + 1, 8)]
                for i in range(k, end):
                    m = cols[i][s] * inv
                    if i == k:
                        m = jnp.where(sub1 > s, m, 0.0)
                    for u in range(s + 1, 8):
                        cols[i][u] = cols[i][u] - m * heads[u - s - 1]
                    rows[i] = rows[i] - wide(m) * row
                scale = jnp.where(sub1 == s, lax.rsqrt(pivot), scale)
            rows[k] = jnp.where((lane < 8 * k + 8) | (lane >= 8 * end), rows[k] * wide(scale), 0.0)
            x_ref[8 * k : 8 * k + 8, :] = jnp.where(lane < 8 * k + 8, rows[k], 0.0)
        if end < blocks:
            v = jnp.concatenate(rows[top:end], axis=0)
            d = lax.dot_general(
                v[:, 8 * end :], v, (((0,), (0,)), ((), ())), precision=lax.Precision.HIGHEST, preferred_element_type=f32
            )
            done = (lane >= 8 * top) & (lane < 8 * end)
            for i in range(end, blocks):
                rows[i] = jnp.where(done, 0.0, rows[i]) - d[8 * (i - end) : 8 * (i - end) + 8, :]
        between(top // group)


def finish_kernel(b_in, w_hbm, x_hbm, b_hbm, f_hbm, w, x, f, b, load, store):
    def move(src, dst, sem):
        k = pltpu.make_async_copy(src, dst, sem)
        k.start()
        return k

    n = ROWS // 2
    x_load = move(x_hbm, x, load.at[4])
    w_load = [move(w_hbm.at[pl.ds(2 * i, 2)], w.at[pl.ds(2 * i, 2)], load.at[i]) for i in range(4)]
    b_load = [move(b_in.at[pl.ds(n * i, n)], b.at[pl.ds(n * i, n)], load.at[5 + i]) for i in range(2)]
    x_load.wait()
    inv = split(x[...])
    stores = []
    for i in range(4):
        lanes = pl.ds(256 * i, 256)
        w_load[i].wait()
        pair = jnp.concatenate([w[2 * i], w[2 * i + 1]], axis=1)
        f[:, lanes] = mm(inv, split(pair), ((1,), (0,)))
        stores.append(move(f.at[:, lanes], f_hbm.at[:, lanes], store.at[i]))
    for i in range(2):
        b_load[i].wait()
        stores.append(move(b.at[pl.ds(n * i, n)], b_hbm.at[pl.ds(n * i, n)], store.at[4 + i]))
    for k in stores:
        k.wait()


def finish(basis, total, inverse):
    V, S = pltpu.VMEM, pltpu.SemaphoreType.DMA
    spec = pl.BlockSpec(memory_space=pl.ANY)
    return pl.pallas_call(
        finish_kernel,
        out_shape=(jax.ShapeDtypeStruct((ROWS, RANK), f32), jax.ShapeDtypeStruct((RANK, D), f32)),
        in_specs=[spec] * 3,
        out_specs=(spec,) * 2,
        scratch_shapes=[V((COLS, RANK, 128), f32), V((RANK, RANK), f32), V((RANK, D), f32), V((ROWS, RANK), f32), S((7,)), S((6,))],
        compiler_params=pltpu.CompilerParams(vmem_limit_bytes=60 << 20),
    )(basis, total, inverse)


def body(sample, test_matrix):
    devices = lax.axis_size("rows") * lax.axis_size("grp")
    basis, total, inverse = sketch_and_sum(sample, test_matrix, float((ROWS * devices) ** 0.5))
    return finish(basis, total, inverse)


def solution(mesh):
    placed = (P(("rows", "grp"), None), P())
    return jax.shard_map(
        body, mesh=mesh, in_specs=placed, out_specs=(P(("rows", "grp"), None), P()), check_vma=False
    )
```

```python
import functools

import jax
import jax.numpy as jnp
from jax import lax
from jax.experimental import pallas as pl
from jax.experimental.pallas import tpu as pltpu
from jax.sharding import PartitionSpec as P

MESH = pl.DeviceIdType.MESH
f32, bf16 = jnp.float32, jnp.bfloat16
NX, NY, NZ = 4, 4, 16
RANK, D, ROWS = 256, 1024, 1024
COLS = D // 128
PLANE = sorted(((a, b) for a in range(NX) for b in range(NY) if a or b), key=lambda v: -min(v[0], NX - v[0]) - min(v[1], NY - v[1]))
RING = sorted(range(1, NZ), key=lambda d: -min(d, NZ - d))
PARTS = 1
PB = COLS // PARTS
PIECE = 8 * PB // NZ


def split(v):
    hi = v.astype(bf16)
    return hi, (v - hi.astype(f32)).astype(bf16)


def mm(a, b, dims):
    def dot(u, v):
        return lax.dot_general(u, v, (dims, ((), ())), preferred_element_type=f32)

    (ah, al), (bh, bl) = a, b
    return dot(ah, bh) + (dot(ah, bl) + dot(al, bh))


def reduce_kernel(s_hbm, t_hbm, b, out, x_ref, sk_ref, s_ref, t_ref, sh, sl, skt, w, core_in, s0, r1, zs, rz, zt, za,
                  gl, gcore_in, gs0, gr1, gz, go, load, ssc, rsc, ssp, rsp, ssz, rsz, scale):
    r = lax.axis_index("rows")
    g = lax.axis_index("grp")
    x, y, z, c = lax.div(r, NZ), lax.div(g, 2), lax.rem(r, NZ), lax.rem(g, 2)
    o = 1 - c

    def at(dx, dy, dz):
        return (lax.rem(x + dx, NX) * NZ + lax.rem(z + dz, NZ), lax.rem(y + dy, NY) * 2 + c)

    partner = (r, y * 2 + o)
    started = []

    def rows(a, n):
        return pl.ds(pl.multiple_of(a, 8), n)

    def send(src, dst, ss, rs, dev):
        k = pltpu.make_async_remote_copy(src_ref=src, dst_ref=dst, send_sem=ss, recv_sem=rs, device_id=dev, device_id_type=MESH)
        k.start()
        started.append(k)
        return k

    def arrive(copies):
        for k in copies:
            k.wait_recv()

    def core_send(phase, src, dst):
        return send(src, dst, ssc.at[phase], rsc.at[phase], partner)

    def plane_send(phase, src, dst):
        copies = []
        for i, (dx, dy) in enumerate(PLANE):
            q = lax.rem(x + dx, NX) * NY + lax.rem(y + dy, NY)
            copies.append(send(src(q), dst(i), ssp.at[phase, i], rsp.at[phase, i], at(dx, dy, 0)))
        return copies

    def z_send(phase, src, dst):
        return [send(src(lax.rem(z + d, NZ)), dst(d), ssz.at[phase, d], rsz.at[phase, d], at(0, 0, d)) for d in RING]

    n = ROWS // 2
    t_load = pltpu.make_async_copy(t_hbm, t_ref, load.at[2])
    t_load.start()
    loads = [pltpu.make_async_copy(s_hbm.at[pl.ds(i * n, n)], s_ref.at[pl.ds(i * n, n)], load.at[i]) for i in range(2)]
    for k in loads:
        k.start()
    barrier = pltpu.get_barrier_semaphore()

    def greet(dev):
        pl.semaphore_signal(barrier, inc=1, device_id=dev, device_id_type=MESH)

    for d in RING:
        greet(at(0, 0, d))
    for dx, dy in PLANE:
        greet(at(dx, dy, 0))
    greet(partner)

    t_load.wait()
    t = split(t_ref[...].T)
    for i in range(2):
        loads[i].wait()
        at_i = pl.ds(i * n, n)
        s = split(s_ref[at_i, :])
        sh[at_i, :], sl[at_i, :] = s
        skt[:, at_i] = mm(t, s, ((1,), (1,)))

    sk = split(skt[...])
    for q in range(4):
        lanes = pl.ds(256 * q, 256)
        d = mm(sk, (sh[:, lanes], sl[:, lanes]), ((1,), (0,)))
        w[2 * q] = d[:, :128]
        w[2 * q + 1] = d[:, 128:]
    whole = jnp.concatenate([w[j] for j in range(COLS)], axis=1)
    gram = mm(split(whole), split(t_ref[...]), ((1,), (0,)))
    gl[0] = gram[:, :128]
    gl[1] = gram[:, 128:]

    mine, theirs = rows(128 * c, 128), rows(128 * o, 128)
    pl.semaphore_wait(barrier, 1 + len(PLANE) + len(RING))
    g_core = core_send(0, gl.at[:, theirs], gcore_in)
    w_core = []
    for h in range(PARTS):
        at_h = pl.ds(PB * h, PB)
        w_core.append(core_send(1 + h, w.at[at_h, theirs], core_in.at[at_h]))

    own = rows(8 * (x * NY + y), 8)
    arrive([g_core])
    gs0[...] = gl[:, mine, :] + gcore_in[...]
    g_plane = plane_send(0, lambda q: gs0.at[:, rows(8 * q, 8)], lambda i: gr1.at[i])
    w_plane = []
    for h in range(PARTS):
        at_h = pl.ds(PB * h, PB)
        arrive(w_core[h : h + 1])
        s0[at_h] = w[at_h, mine, :] + core_in[at_h]
        w_plane.append(plane_send(1 + h, lambda q: s0.at[at_h, rows(8 * q, 8)], lambda i: r1.at[h, i]))
    sk_ref[...] = skt[...].T

    arrive(g_plane)
    v = gs0[:, own, :]
    for i in range(len(PLANE)):
        v = v + gr1[i]
    gz[z] = v
    g_z = z_send(0, lambda q: gz.at[z], lambda d: gz.at[z])

    w_z = []
    for h in range(PARTS):
        arrive(w_plane[h])
        v = s0[pl.ds(PB * h, PB), own, :]
        for i in range(len(PLANE)):
            v = v + r1[h, i]
        for j in range(PB):
            for p in range(8 // PIECE):
                zs[h, j * (8 // PIECE) + p] = v[j, p * PIECE : (p + 1) * PIECE]
        w_z.append(z_send(1 + h, lambda q: zs.at[h, q], lambda d: rz.at[h, d]))

    arrive(g_z)
    v = gz[0]
    for d in range(1, NZ):
        v = v + gz[d]
    place = rows(128 * c + 8 * (x * NY + y), 8)
    go[:, place, :] = v
    g_back = plane_send(1 + PARTS, lambda q: go.at[:, place], lambda i: go.at[:, place])

    w_all = []
    for h in range(PARTS):
        arrive(w_z[h])
        v = zs[h, z]
        for d in RING:
            v = v + rz[h, d]
        zt[h] = v
        za[h, z] = v
        w_all.append(z_send(1 + PARTS + h, lambda q: zt.at[h], lambda d: za.at[h, z]))

    arrive(g_back)
    arrive([core_send(1 + PARTS, go.at[:, mine], go.at[:, mine])])

    w_back = []

    def between(i):
        if i != 0:
            return
        for h in range(PARTS):
            arrive(w_all[h])
            for j in range(PB):
                k = 8 // PIECE
                out[PB * h + j, place, :] = jnp.concatenate([za[h, j * k + p] for p in range(k)], axis=0)
            ref = out.at[pl.ds(PB * h, PB), place]
            w_back.append(plane_send(2 + PARTS + h, lambda q: ref, lambda d: ref))

    blocks = [jnp.concatenate([go[0, 8 * i : 8 * i + 8, :], go[1, 8 * i : 8 * i + 8, :]], axis=1) for i in range(RANK // 8)]
    inverse_factor(blocks, x_ref, between)

    turned = split(x_ref[...].T)
    n = ROWS // 4
    for i in range(4):
        at_i = pl.ds(n * i, n)
        b[at_i, :] = mm(split(sk_ref[at_i, :]), turned, ((1,), (0,))) * scale
    last = []
    for h in range(PARTS):
        arrive(w_back[h])
        ref = out.at[pl.ds(PB * h, PB), mine]
        last.append(core_send(2 + PARTS + h, ref, ref))
    arrive(last)
    for k in started:
        k.wait_send()


def sketch_and_sum(sample, test_matrix, scale):
    V, S = pltpu.VMEM, pltpu.SemaphoreType.DMA
    n = len(PLANE)
    spec = pl.BlockSpec(memory_space=pl.ANY)
    return pl.pallas_call(
        functools.partial(reduce_kernel, scale=scale),
        out_shape=(
            V((ROWS, RANK), f32),
            V((COLS, RANK, 128), f32),
            V((RANK, RANK), f32),
        ),
        in_specs=[spec] * 2,
        out_specs=(pl.BlockSpec(memory_space=V),) * 3,
        scratch_shapes=[
            V((ROWS, RANK), f32),
            V((ROWS, D), f32), V((D, RANK), f32), V((ROWS, D), bf16), V((ROWS, D), bf16), V((RANK, ROWS), f32),
            V((COLS, RANK, 128), f32), V((COLS, 128, 128), f32), V((COLS, 128, 128), f32), V((PARTS, n, PB, 8, 128), f32),
            V((PARTS, NZ, PIECE, 128), f32), V((PARTS, NZ, PIECE, 128), f32), V((PARTS, PIECE, 128), f32),
            V((PARTS, NZ, PIECE, 128), f32),
            V((2, RANK, 128), f32), V((2, 128, 128), f32), V((2, 128, 128), f32), V((n, 2, 8, 128), f32),
            V((NZ, 2, 8, 128), f32), V((2, RANK, 128), f32),
            S((3,)), S((2 + 2 * PARTS,)), S((2 + 2 * PARTS,)), S((2 + 2 * PARTS, n)), S((2 + 2 * PARTS, n)),
            S((1 + 2 * PARTS, NZ)), S((1 + 2 * PARTS, NZ)),
        ],
        compiler_params=pltpu.CompilerParams(collective_id=0, has_side_effects=True, vmem_limit_bytes=61 << 20),
    )(sample, test_matrix)


def inverse_factor(rows, x_ref, between, group=8):
    n = RANK
    lane = lax.broadcasted_iota(jnp.int32, (8, n), 1)
    sub = lax.broadcasted_iota(jnp.int32, (8, n), 0)
    sub1 = lax.broadcasted_iota(jnp.int32, (8, 128), 0)
    blocks = n // 8

    def wide(v):
        return jnp.concatenate([v] * (n // 128), axis=1)

    for top in range(0, blocks, group):
        end = top + group
        for k in range(top, end):
            own = (lane >= 8 * k) & (lane < 8 * k + 8)
            cols = {}
            for i in range(k, end):
                cols[i] = [jnp.broadcast_to(rows[i][:, 8 * k + s : 8 * k + s + 1], (8, 128)) for s in range(8)]
                rows[i] = jnp.where(own, (lane - 8 * k == sub).astype(f32) if i == k else 0.0, rows[i])
            scale = jnp.zeros((8, 128), f32)
            for s in range(8):
                pivot = jnp.broadcast_to(cols[k][s][s : s + 1, :], (8, 128))
                inv = 1.0 / pivot
                row = jnp.broadcast_to(rows[k][s : s + 1, :], (8, n))
                heads = [jnp.broadcast_to(cols[k][u][s : s + 1, :], (8, 128)) for u in range(s + 1, 8)]
                for i in range(k, end):
                    m = cols[i][s] * inv
                    if i == k:
                        m = jnp.where(sub1 > s, m, 0.0)
                    for u in range(s + 1, 8):
                        cols[i][u] = cols[i][u] - m * heads[u - s - 1]
                    rows[i] = rows[i] - wide(m) * row
                scale = jnp.where(sub1 == s, lax.rsqrt(pivot), scale)
            rows[k] = jnp.where((lane < 8 * k + 8) | (lane >= 8 * end), rows[k] * wide(scale), 0.0)
            x_ref[8 * k : 8 * k + 8, :] = jnp.where(lane < 8 * k + 8, rows[k], 0.0)
        if end < blocks:
            v = jnp.concatenate(rows[top:end], axis=0)
            d = lax.dot_general(
                v[:, 8 * end :], v, (((0,), (0,)), ((), ())), precision=lax.Precision.HIGHEST, preferred_element_type=f32
            )
            done = (lane >= 8 * top) & (lane < 8 * end)
            for i in range(end, blocks):
                rows[i] = jnp.where(done, 0.0, rows[i]) - d[8 * (i - end) : 8 * (i - end) + 8, :]
        between(top // group)


def finish_kernel(b, w, x, b_hbm, f_hbm, f, store):
    def give(src, dst, i):
        k = pltpu.make_async_copy(src, dst, store.at[i])
        k.start()
        return k

    stores = [give(b, b_hbm, 4)]
    inv = split(x[...])
    for i in range(4):
        lanes = pl.ds(256 * i, 256)
        pair = jnp.concatenate([w[2 * i], w[2 * i + 1]], axis=1)
        f[:, lanes] = mm(inv, split(pair), ((1,), (0,)))
        stores.append(give(f.at[:, lanes], f_hbm.at[:, lanes], i))
    for k in stores:
        k.wait()


def finish(basis, total, inverse):
    V, S = pltpu.VMEM, pltpu.SemaphoreType.DMA
    return pl.pallas_call(
        finish_kernel,
        out_shape=(jax.ShapeDtypeStruct((ROWS, RANK), f32), jax.ShapeDtypeStruct((RANK, D), f32)),
        in_specs=[pl.BlockSpec(memory_space=V)] * 3,
        out_specs=(pl.BlockSpec(memory_space=pl.ANY),) * 2,
        scratch_shapes=[V((RANK, D), f32), S((5,))],
        compiler_params=pltpu.CompilerParams(vmem_limit_bytes=24 << 20),
    )(basis, total, inverse)


def body(sample, test_matrix):
    devices = lax.axis_size("rows") * lax.axis_size("grp")
    basis, total, inverse = sketch_and_sum(sample, test_matrix, float((ROWS * devices) ** 0.5))
    return finish(basis, total, inverse)


def solution(mesh):
    placed = (P(("rows", "grp"), None), P())
    return jax.shard_map(
        body, mesh=mesh, in_specs=placed, out_specs=(P(("rows", "grp"), None), P()), check_vma=False
    )
```

```python
import functools

import jax
import jax.numpy as jnp
from jax import lax
from jax.experimental import pallas as pl
from jax.experimental.pallas import tpu as pltpu
from jax.sharding import PartitionSpec as P

MESH = pl.DeviceIdType.MESH
f32, bf16 = jnp.float32, jnp.bfloat16
NX, NY, NZ = 4, 4, 16
RANK, D, ROWS = 256, 1024, 1024
COLS = D // 128
PLANE = sorted(((a, b) for a in range(NX) for b in range(NY) if a or b), key=lambda v: -min(v[0], NX - v[0]) - min(v[1], NY - v[1]))
RING = sorted(range(1, NZ), key=lambda d: -min(d, NZ - d))
PARTS = 1
PB = COLS // PARTS
PIECE = 8 * PB // NZ


def split(v):
    hi = v.astype(bf16)
    return hi, (v - hi.astype(f32)).astype(bf16)


def mm(a, b, dims):
    def dot(u, v):
        return lax.dot_general(u, v, (dims, ((), ())), preferred_element_type=f32)

    (ah, al), (bh, bl) = a, b
    return dot(ah, bh) + (dot(ah, bl) + dot(al, bh))


def reduce_kernel(s_hbm, t_hbm, b, out, x_ref, sk_ref, s_ref, t_ref, sh, sl, skt, w, core_in, s0, r1, zs, rz, zt, za,
                  gl, gcore_in, gs0, gr1, gz, go, load, ssc, rsc, ssp, rsp, ssz, rsz, scale):
    r = lax.axis_index("rows")
    g = lax.axis_index("grp")
    x, y, z, c = lax.div(r, NZ), lax.div(g, 2), lax.rem(r, NZ), lax.rem(g, 2)
    o = 1 - c

    def at(dx, dy, dz):
        return (lax.rem(x + dx, NX) * NZ + lax.rem(z + dz, NZ), lax.rem(y + dy, NY) * 2 + c)

    partner = (r, y * 2 + o)
    started = []

    def rows(a, n):
        return pl.ds(pl.multiple_of(a, 8), n)

    def send(src, dst, ss, rs, dev):
        k = pltpu.make_async_remote_copy(src_ref=src, dst_ref=dst, send_sem=ss, recv_sem=rs, device_id=dev, device_id_type=MESH)
        k.start()
        started.append(k)
        return k

    def arrive(copies):
        for k in copies:
            k.wait_recv()

    def core_send(phase, src, dst):
        return send(src, dst, ssc.at[phase], rsc.at[phase], partner)

    def plane_send(phase, src, dst):
        copies = []
        for i, (dx, dy) in enumerate(PLANE):
            q = lax.rem(x + dx, NX) * NY + lax.rem(y + dy, NY)
            copies.append(send(src(q), dst(i), ssp.at[phase, i], rsp.at[phase, i], at(dx, dy, 0)))
        return copies

    def z_send(phase, src, dst):
        return [send(src(lax.rem(z + d, NZ)), dst(d), ssz.at[phase, d], rsz.at[phase, d], at(0, 0, d)) for d in RING]

    n = ROWS // 2
    t_load = pltpu.make_async_copy(t_hbm, t_ref, load.at[2])
    t_load.start()
    loads = [pltpu.make_async_copy(s_hbm.at[pl.ds(i * n, n)], s_ref.at[pl.ds(i * n, n)], load.at[i]) for i in range(2)]
    for k in loads:
        k.start()
    barrier = pltpu.get_barrier_semaphore()

    def greet(dev):
        pl.semaphore_signal(barrier, inc=1, device_id=dev, device_id_type=MESH)

    for d in RING:
        greet(at(0, 0, d))

    t_load.wait()
    t = split(t_ref[...].T)
    for dx, dy in PLANE:
        greet(at(dx, dy, 0))
    greet(partner)
    for i in range(2):
        loads[i].wait()
        at_i = pl.ds(i * n, n)
        s = split(s_ref[at_i, :])
        sh[at_i, :], sl[at_i, :] = s
        skt[:, at_i] = mm(t, s, ((1,), (1,)))

    sk = split(skt[...])
    sk_ref[...] = skt[...].T
    gram = mm(sk, split(sk_ref[...]), ((1,), (0,)))
    gl[0] = gram[:, :128]
    gl[1] = gram[:, 128:]
    mine, theirs = rows(128 * c, 128), rows(128 * o, 128)
    pl.semaphore_wait(barrier, 1 + len(PLANE) + len(RING))
    g_core = core_send(0, gl.at[:, theirs], gcore_in)

    for q in range(4):
        lanes = pl.ds(256 * q, 256)
        d = mm(sk, (sh[:, lanes], sl[:, lanes]), ((1,), (0,)))
        w[2 * q] = d[:, :128]
        w[2 * q + 1] = d[:, 128:]
    w_core = []
    for h in range(PARTS):
        at_h = pl.ds(PB * h, PB)
        w_core.append(core_send(1 + h, w.at[at_h, theirs], core_in.at[at_h]))

    own = rows(8 * (x * NY + y), 8)
    arrive([g_core])
    gs0[...] = gl[:, mine, :] + gcore_in[...]
    g_plane = plane_send(0, lambda q: gs0.at[:, rows(8 * q, 8)], lambda i: gr1.at[i])
    w_plane = []
    for h in range(PARTS):
        at_h = pl.ds(PB * h, PB)
        arrive(w_core[h : h + 1])
        s0[at_h] = w[at_h, mine, :] + core_in[at_h]
        w_plane.append(plane_send(1 + h, lambda q: s0.at[at_h, rows(8 * q, 8)], lambda i: r1.at[h, i]))

    arrive(g_plane)
    v = gs0[:, own, :]
    for i in range(len(PLANE)):
        v = v + gr1[i]
    gz[z] = v
    g_z = z_send(0, lambda q: gz.at[z], lambda d: gz.at[z])

    w_z = []
    for h in range(PARTS):
        arrive(w_plane[h])
        v = s0[pl.ds(PB * h, PB), own, :]
        for i in range(len(PLANE)):
            v = v + r1[h, i]
        for j in range(PB):
            for p in range(8 // PIECE):
                zs[h, j * (8 // PIECE) + p] = v[j, p * PIECE : (p + 1) * PIECE]
        w_z.append(z_send(1 + h, lambda q: zs.at[h, q], lambda d: rz.at[h, d]))

    arrive(g_z)
    v = gz[0]
    for d in range(1, NZ):
        v = v + gz[d]
    place = rows(128 * c + 8 * (x * NY + y), 8)
    go[:, place, :] = v
    g_back = plane_send(1 + PARTS, lambda q: go.at[:, place], lambda i: go.at[:, place])

    w_all = []
    for h in range(PARTS):
        arrive(w_z[h])
        v = zs[h, z]
        for d in RING:
            v = v + rz[h, d]
        zt[h] = v
        za[h, z] = v
        w_all.append(z_send(1 + PARTS + h, lambda q: zt.at[h], lambda d: za.at[h, z]))

    arrive(g_back)
    arrive([core_send(1 + PARTS, go.at[:, mine], go.at[:, mine])])

    w_back = []

    def between(i):
        if i != 0:
            return
        for h in range(PARTS):
            arrive(w_all[h])
            for j in range(PB):
                k = 8 // PIECE
                out[PB * h + j, place, :] = jnp.concatenate([za[h, j * k + p] for p in range(k)], axis=0)
            ref = out.at[pl.ds(PB * h, PB), place]
            w_back.append(plane_send(2 + PARTS + h, lambda q: ref, lambda d: ref))

    blocks = [jnp.concatenate([go[0, 8 * i : 8 * i + 8, :], go[1, 8 * i : 8 * i + 8, :]], axis=1) for i in range(RANK // 8)]
    inverse_factor(blocks, x_ref, between)

    last = []
    for h in range(PARTS):
        arrive(w_back[h])
        ref = out.at[pl.ds(PB * h, PB), mine]
        last.append(core_send(2 + PARTS + h, ref, ref))
    turned = split(x_ref[...].T)
    n = ROWS // 4
    for i in range(4):
        at_i = pl.ds(n * i, n)
        b[at_i, :] = mm(split(sk_ref[at_i, :]), turned, ((1,), (0,))) * scale
    arrive(last)
    for k in started:
        k.wait_send()


def sketch_and_sum(sample, test_matrix, scale):
    V, S = pltpu.VMEM, pltpu.SemaphoreType.DMA
    n = len(PLANE)
    spec = pl.BlockSpec(memory_space=pl.ANY)
    return pl.pallas_call(
        functools.partial(reduce_kernel, scale=scale),
        out_shape=(
            V((ROWS, RANK), f32),
            V((COLS, RANK, 128), f32),
            V((RANK, RANK), f32),
        ),
        in_specs=[spec] * 2,
        out_specs=(pl.BlockSpec(memory_space=V),) * 3,
        scratch_shapes=[
            V((ROWS, RANK), f32),
            V((ROWS, D), f32), V((D, RANK), f32), V((ROWS, D), bf16), V((ROWS, D), bf16), V((RANK, ROWS), f32),
            V((COLS, RANK, 128), f32), V((COLS, 128, 128), f32), V((COLS, 128, 128), f32), V((PARTS, n, PB, 8, 128), f32),
            V((PARTS, NZ, PIECE, 128), f32), V((PARTS, NZ, PIECE, 128), f32), V((PARTS, PIECE, 128), f32),
            V((PARTS, NZ, PIECE, 128), f32),
            V((2, RANK, 128), f32), V((2, 128, 128), f32), V((2, 128, 128), f32), V((n, 2, 8, 128), f32),
            V((NZ, 2, 8, 128), f32), V((2, RANK, 128), f32),
            S((3,)), S((2 + 2 * PARTS,)), S((2 + 2 * PARTS,)), S((2 + 2 * PARTS, n)), S((2 + 2 * PARTS, n)),
            S((1 + 2 * PARTS, NZ)), S((1 + 2 * PARTS, NZ)),
        ],
        compiler_params=pltpu.CompilerParams(collective_id=0, has_side_effects=True, vmem_limit_bytes=61 << 20),
    )(sample, test_matrix)


def inverse_factor(rows, x_ref, between, group=8):
    n = RANK
    lane = lax.broadcasted_iota(jnp.int32, (8, n), 1)
    sub = lax.broadcasted_iota(jnp.int32, (8, n), 0)
    sub1 = lax.broadcasted_iota(jnp.int32, (8, 128), 0)
    blocks = n // 8

    def wide(v):
        return jnp.concatenate([v] * (n // 128), axis=1)

    for top in range(0, blocks, group):
        end = top + group
        for k in range(top, end):
            own = (lane >= 8 * k) & (lane < 8 * k + 8)
            cols = {}
            for i in range(k, end):
                cols[i] = [jnp.broadcast_to(rows[i][:, 8 * k + s : 8 * k + s + 1], (8, 128)) for s in range(8)]
                rows[i] = jnp.where(own, (lane - 8 * k == sub).astype(f32) if i == k else 0.0, rows[i])
            scale = jnp.zeros((8, 128), f32)
            for s in range(8):
                pivot = jnp.broadcast_to(cols[k][s][s : s + 1, :], (8, 128))
                inv = 1.0 / pivot
                row = jnp.broadcast_to(rows[k][s : s + 1, :], (8, n))
                heads = [jnp.broadcast_to(cols[k][u][s : s + 1, :], (8, 128)) for u in range(s + 1, 8)]
                for i in range(k, end):
                    m = cols[i][s] * inv
                    if i == k:
                        m = jnp.where(sub1 > s, m, 0.0)
                    for u in range(s + 1, 8):
                        cols[i][u] = cols[i][u] - m * heads[u - s - 1]
                    rows[i] = rows[i] - wide(m) * row
                scale = jnp.where(sub1 == s, lax.rsqrt(pivot), scale)
            rows[k] = jnp.where((lane < 8 * k + 8) | (lane >= 8 * end), rows[k] * wide(scale), 0.0)
            x_ref[8 * k : 8 * k + 8, :] = jnp.where(lane < 8 * k + 8, rows[k], 0.0)
        if end < blocks:
            v = jnp.concatenate(rows[top:end], axis=0)
            d = lax.dot_general(
                v[:, 8 * end :], v, (((0,), (0,)), ((), ())), precision=lax.Precision.HIGHEST, preferred_element_type=f32
            )
            done = (lane >= 8 * top) & (lane < 8 * end)
            for i in range(end, blocks):
                rows[i] = jnp.where(done, 0.0, rows[i]) - d[8 * (i - end) : 8 * (i - end) + 8, :]
        between(top // group)


def finish_kernel(b, w, x, b_hbm, f_hbm, f, store):
    def give(src, dst, i):
        k = pltpu.make_async_copy(src, dst, store.at[i])
        k.start()
        return k

    stores = [give(b, b_hbm, 4)]
    inv = split(x[...])
    for i in range(4):
        lanes = pl.ds(256 * i, 256)
        pair = jnp.concatenate([w[2 * i], w[2 * i + 1]], axis=1)
        f[:, lanes] = mm(inv, split(pair), ((1,), (0,)))
        stores.append(give(f.at[:, lanes], f_hbm.at[:, lanes], i))
    for k in stores:
        k.wait()


def finish(basis, total, inverse):
    V, S = pltpu.VMEM, pltpu.SemaphoreType.DMA
    return pl.pallas_call(
        finish_kernel,
        out_shape=(jax.ShapeDtypeStruct((ROWS, RANK), f32), jax.ShapeDtypeStruct((RANK, D), f32)),
        in_specs=[pl.BlockSpec(memory_space=V)] * 3,
        out_specs=(pl.BlockSpec(memory_space=pl.ANY),) * 2,
        scratch_shapes=[V((RANK, D), f32), S((5,))],
        compiler_params=pltpu.CompilerParams(vmem_limit_bytes=24 << 20),
    )(basis, total, inverse)


def body(sample, test_matrix):
    devices = lax.axis_size("rows") * lax.axis_size("grp")
    basis, total, inverse = sketch_and_sum(sample, test_matrix, float((ROWS * devices) ** 0.5))
    return finish(basis, total, inverse)


def solution(mesh):
    placed = (P(("rows", "grp"), None), P())
    return jax.shard_map(
        body, mesh=mesh, in_specs=placed, out_specs=(P(("rows", "grp"), None), P()), check_vma=False
    )
```
